512 devices in a mesh: ctx: 64 (over y, x, core), tp: 8 (over z).
Axes of the slice: x: 4, y: 8, z: 8, core: 2. Of those that a mesh axis runs over, the one named last changes fastest.
Arguments:
- q_pre: bfloat16 [16384, 5120], P('ctx', 'tp'), may hold values from -360 to 360, as said below
- k_pre: bfloat16 [16384, 5120], P('ctx', 'tp'), may hold values from -360 to 360, as said below
- values: bfloat16 [16384, 5120], P('ctx', 'tp'), may hold values from -6 to 6
- q_gain: float32 [5120], P('tp'), may hold values from 0.1 to 1.9
- k_gain: float32 [5120], P('tp'), may hold values from 0.1 to 1.9
- grad_out: bfloat16 [16384, 5120], P('ctx', 'tp'), may hold values from -6 to 6
- far_frames: int32 [64, 6], P('ctx'), may hold values from 0 to 63, as said below
- far_blocks: int32 [64, 6], P('ctx'), may hold values from 0 to 1, as said below
Outputs:
- attn_out: bfloat16 [16384, 5120], P('ctx', 'tp')
- dq_pre: bfloat16 [16384, 5120], P('ctx', 'tp')
- dk_pre: bfloat16 [16384, 5120], P('ctx', 'tp')
- dv: bfloat16 [16384, 5120], P('ctx', 'tp')
- dq_gain: float32 [5120], P('tp')
- dk_gain: float32 [5120], P('tp')
The draws below stay inside these ranges and needn't reach their ends.
Inputs may be any that keep to these rules, and one draw needn't show every extreme that they name: far_frames[f, j] is f + 2^j or f - 2^j, the one that lies in 0 to 63 where only one does. `far_blocks`: a block index within the frame. `q_pre`: real feature values. `k_pre`: real feature values.
All inputs are finite; a program needn't handle non-finite values.
Results may differ from the reference program's by a relative error of at most 0.009.
The reference program's roundings to bfloat16 on the way count: a program that leaves them out, or rounds other values in their place, can miss the bound.
Values may be sent and summed in bfloat16 or wider, within the bound.
No kernel may reach another device: no remote copies, remote signals or barrier semaphores. Data moves between devices by JAX's collectives and lax.ppermute only.
A program may use at most 64 MiB of HBM per device.

```python
import jax
import jax.numpy as jnp
from jax import lax

HD = 128
HEADS = 40
BLK = 128
FB = 2
NFRAMES = 64
BANDS = 6
TOKENS = 16384


def radial_picks(seed_key):
    frame_ids = jnp.arange(NFRAMES, dtype=jnp.int32)[:, None]
    strides = (2 ** jnp.arange(BANDS, dtype=jnp.int32))[None, :]
    side_key, block_key = jax.random.split(seed_key)
    coin_flip = jax.random.randint(side_key, (NFRAMES, BANDS), 0, 2)
    ahead_frame = frame_ids + strides
    behind = frame_ids - strides
    go_ahead = jnp.where(ahead_frame >= NFRAMES, 0, jnp.where(behind < 0, 1, coin_flip))
    picked = jnp.where(go_ahead == 1, ahead_frame, behind).astype(jnp.int32)
    blocks = jax.random.randint(block_key, (NFRAMES, BANDS), 0, FB).astype(jnp.int32)
    blocks = blocks.at[0, 0].set(FB - 1).at[NFRAMES - 1, 0].set(0)
    return (picked, blocks)


def draw_far_frames(key, part):
    return radial_picks(key)[0]


def draw_far_blocks(key, part):
    return radial_picks(key)[1]


def column_rise(spread):
    position = jnp.arange(HEADS * HD, dtype=jnp.float32) / (HEADS * HD)
    return jnp.exp(spread * position)[None, :]


def draw_q_pre(key, part):
    key = jax.random.fold_in(key, 17)
    private = jnp.clip(jax.random.normal(key, (TOKENS, HEADS * HD), jnp.float32), -6.0, 6.0)
    return (private * column_rise(0.55)).astype(jnp.bfloat16)


def draw_k_pre(key, part):
    key = jax.random.fold_in(key, 29)
    private = jnp.clip(jax.random.normal(key, (TOKENS, HEADS * HD), jnp.float32), -6.0, 6.0)
    return (private * column_rise(0.55)).astype(jnp.bfloat16)


def steps_of(stream_key, shape, pieces, smallest, high):
    def one(dim, shards_of):
        draws = jax.random.uniform(jax.random.fold_in(jax.random.fold_in(stream_key, 6), dim), (shards_of,), jnp.float32, smallest / len(pieces), high / len(pieces))
        return jnp.repeat(jnp.exp(draws), shape[dim] // shards_of).reshape((-1,) + (1,) * (len(shape) - dim - 1))

    loudness = one(*pieces[0])
    for cut in pieces[1:]:
        loudness = loudness * one(*cut)
    return loudness


def centred(own_key, extent, deviation, limit, shards=(), kind=jnp.bfloat16):
    factor_of = steps_of(own_key, extent, shards, -0.22, 0.18) if shards else 1.0
    values = jax.random.normal(own_key, extent, jnp.float32) * deviation * factor_of
    return jnp.minimum(jnp.maximum(values, -limit), limit).astype(kind)


def setup_inputs(seed: int = 0) -> dict:
    seeds = jax.random.split(jax.random.key(seed), 9)
    q_pre = draw_q_pre(jax.random.fold_in(seeds[8], 71), 0)
    k_pre = draw_k_pre(jax.random.fold_in(seeds[8], 71), 0)
    values = centred(seeds[2], (TOKENS, HEADS * HD), 1.0, 6.0, ((0, 64), (1, 8)))
    q_gain = jnp.clip(1.0 + 0.18 * jax.random.normal(seeds[3], (HEADS * HD,), jnp.float32), 0.1, 1.9)
    k_gain = jnp.clip(1.0 + 0.18 * jax.random.normal(seeds[4], (HEADS * HD,), jnp.float32), 0.1, 1.9)
    grad_out = centred(seeds[5], (TOKENS, HEADS * HD), 1.0, 6.0, ((0, 64), (1, 8)))
    far_frames = draw_far_frames(jax.random.fold_in(seeds[8], 71), 0)
    far_blocks = draw_far_blocks(jax.random.fold_in(seeds[8], 71), 0)
    return dict(q_pre=q_pre, k_pre=k_pre, values=values, q_gain=q_gain, k_gain=k_gain, grad_out=grad_out, far_frames=far_frames, far_blocks=far_blocks)


EPS = 1e-06

def round_half(x):
    return lax.optimization_barrier(x.astype(jnp.bfloat16)).astype(jnp.float32)

def normalize(pre, gain):
    pre_float = pre.astype(jnp.float32)
    rstd = lax.rsqrt(lax.optimization_barrier(jnp.mean(pre_float * pre_float, axis=1, keepdims=True)) + EPS)
    return (pre_float, rstd, (pre_float * rstd * gain).astype(jnp.bfloat16))

def norm_backward(pre_float, rstd, gain, grad_normed):
    col_count = pre_float.shape[1]
    inner = lax.optimization_barrier(jnp.sum(grad_normed * gain * pre_float, axis=1, keepdims=True))
    grad_pre = rstd * gain * grad_normed - pre_float * rstd * rstd * rstd * inner / col_count
    grad_gain = lax.optimization_barrier(jnp.sum(grad_normed * pre_float * rstd, axis=0))
    return (grad_pre.astype(jnp.bfloat16), grad_gain)

def reference(q_pre, k_pre, values, q_gain, k_gain, grad_out, far_frames, far_blocks):
    col_count = q_pre.shape[1]
    head_count = col_count // HD
    softmax_scale = HD ** (-0.5)
    frame_rows = FB * BLK
    q_float, q_rstd, q_normed = normalize(q_pre, q_gain)
    k_float, k_rstd, k_normed = normalize(k_pre, k_gain)
    query_frames = q_normed.reshape(NFRAMES, frame_rows, head_count, HD)
    grad_frames = grad_out.reshape(NFRAMES, frame_rows, head_count, HD)
    key_blocks = k_normed.reshape(NFRAMES * FB, BLK, head_count, HD)
    value_blocks = values.reshape(NFRAMES * FB, BLK, head_count, HD)
    far_ids = (far_frames * FB + far_blocks).astype(jnp.int32)
    own_offsets = jnp.arange(FB, dtype=jnp.int32)

    def one_frame(carry, frame_index):
        key_grads, value_grads = carry
        own_ids = (frame_index * FB + own_offsets).astype(jnp.int32)
        my_far = far_ids[frame_index]
        block_ids = jnp.concatenate([own_ids, my_far])
        keys = key_blocks[block_ids].reshape(-1, head_count, HD).astype(jnp.float32)
        vals = value_blocks[block_ids].reshape(-1, head_count, HD).astype(jnp.float32)
        queries = query_frames[frame_index].astype(jnp.float32)
        grads = grad_frames[frame_index].astype(jnp.float32)
        scores = jnp.einsum('qhd,khd->hqk', queries, keys) * softmax_scale
        top = lax.optimization_barrier(jnp.max(scores, axis=2, keepdims=True))
        log_total = top + jnp.log(lax.optimization_barrier(jnp.sum(jnp.exp(scores - top), axis=2, keepdims=True)))
        probs = jnp.exp(scores - log_total)
        probs_half = round_half(probs)
        attn = jnp.einsum('hqk,khd->qhd', probs_half, vals).astype(jnp.bfloat16)
        delta = jnp.einsum('qhd,qhd->hq', grads, attn.astype(jnp.float32))[:, :, None]
        dprobs = jnp.einsum('qhd,khd->hqk', grads, vals)
        dscores = round_half(probs * (dprobs - delta))
        query_grad = jnp.einsum('hqk,khd->qhd', dscores, keys) * softmax_scale
        key_part = jnp.einsum('hqk,qhd->khd', dscores, queries) * softmax_scale
        value_part = jnp.einsum('hqk,qhd->khd', probs_half, grads)
        key_part = key_part.reshape(FB + BANDS, BLK, head_count, HD)
        value_part = value_part.reshape(FB + BANDS, BLK, head_count, HD)
        key_grads = key_grads.at[own_ids].add(key_part[:FB]).at[my_far].add(round_half(key_part[FB:]))
        value_grads = value_grads.at[own_ids].add(value_part[:FB]).at[my_far].add(round_half(value_part[FB:]))
        return ((key_grads, value_grads), (attn, query_grad))
    zeros = jnp.zeros((NFRAMES * FB, BLK, head_count, HD), jnp.float32)
    (key_grads, value_grads), (attn, query_grad) = lax.scan(one_frame, (zeros, zeros), jnp.arange(NFRAMES, dtype=jnp.int32))
    attn_out = attn.reshape(TOKENS, col_count)
    dq_pre, dq_gain = norm_backward(q_float, q_rstd, q_gain, query_grad.reshape(TOKENS, col_count))
    dk_pre, dk_gain = norm_backward(k_float, k_rstd, k_gain, key_grads.reshape(TOKENS, col_count))
    dv = value_grads.reshape(TOKENS, col_count).astype(jnp.bfloat16)
    return (attn_out, dq_pre, dk_pre, dv, dq_gain, dk_gain)
```

```python
import functools

import jax
import jax.numpy as jnp
from jax import lax
from jax.experimental import pallas as pl
from jax.experimental.pallas import tpu as pltpu
from jax.sharding import Mesh
from jax.sharding import PartitionSpec as P

HD = 128
BLK = 128
EPS = 1e-06
SCALE = HD**-0.5
LOG2E = 1.4426950408889634
CTX = ("cy", "cx")
WAYS = tuple((band, other) for band in range(6) for other in range(2 if band < 5 else 1))
MIB = 1 << 20


ORDER = ((4, 0), (4, 1), (5, 0), (2, 0), (2, 1), (3, 0), (3, 1), (1, 0), (1, 1), (0, 0), (0, 1))
WINDOW = 5


def pairs_of(way, count=64):
    band, other = way
    stride = 1 << band
    lower = [f for f in range(count - stride) if (f >> band) & 1 == other]
    return [pair for f in lower for pair in ((f, f + stride), (f + stride, f))]


def move(value, way):
    return lax.ppermute(value, CTX, pairs_of(way))


def dot(a, b, dims):
    return lax.dot_general(a, b, (dims, ((), ())), preferred_element_type=jnp.float32)


def rows_to_lanes(tile):
    return jnp.sum(tile.T, axis=0, keepdims=True)


def lanes_to_rows(row):
    return jnp.broadcast_to(row, (HD, row.shape[1])).T


def square_kernel(q_ref, k_ref, out_ref):
    for i, ref in enumerate((q_ref, k_ref)):
        rows, cols = ref.shape
        total = jnp.zeros((rows, HD), jnp.float32)
        for c in range(0, cols, HD):
            x = ref[:, c : c + HD].astype(jnp.float32)
            total += x * x
        out_ref[:, i * rows : (i + 1) * rows] = rows_to_lanes(total)


def slot_of(note):
    return pl.multiple_of(((note + 1) & 1) * BLK, BLK)


BIT = 8


def is_reader(mine, notes, i):
    band, other = WAYS[i]
    note = notes[i]
    if band == 5:
        return note >= 1
    bit = mine[BIT + band]
    return (note >= 1) & ((note >= 3).astype(jnp.int32) == (1 - bit if other else bit))


def notes_kernel(place, frames, blocks, first_ref, second_ref, mine):
    half = place[1] // 2
    bands = frames.shape[1]
    for ref, band in ((first_ref, half), (second_ref, jnp.minimum(half + 4, bands - 1))):
        code = 1 + blocks[0, band] + 2 * (frames[0, band] > place[0]).astype(jnp.int32)
        ref[...] = jnp.full((1, HD), code, jnp.int32).astype(jnp.float32)
    for j in range(bands):
        mine[j] = (frames[0, j] > place[0]).astype(jnp.int32)
        mine[BIT + j] = (place[0] >> j) & 1


def norm_kernel(width, notes, sums_ref, qg_ref, kg_ref, q_ref, k_ref, v_ref, qn_ref, kn_ref, *sends):
    rows, cols = q_ref.shape
    rstd = lax.rsqrt(sums_ref[...] / width + EPS)
    q_rstd = lanes_to_rows(rstd[:, :rows])
    k_rstd = lanes_to_rows(rstd[:, rows:])
    for c in range(0, cols, HD):
        at = slice(c, c + HD)
        qn_ref[:, at] = (q_ref[:, at].astype(jnp.float32) * q_rstd * qg_ref[:, at]).astype(jnp.bfloat16)
        kn_ref[:, at] = (k_ref[:, at].astype(jnp.float32) * k_rstd * kg_ref[:, at]).astype(jnp.bfloat16)
    for i, send in enumerate(sends):
        start = slot_of(notes[i])
        send[0] = kn_ref[pl.ds(start, BLK), :]
        send[1] = v_ref[pl.ds(start, BLK), :]


def attention_kernel(width, mine, sums_ref, qg_ref, kg_ref, q_ref, k_ref, v_ref, do_ref, qpre_ref, *refs):
    recv = dict(zip(ORDER, refs[: len(WAYS)]))
    out_ref, dq_ref, dk_ref, dv_ref, inner_ref, gains_ref = refs[len(WAYS) : len(WAYS) + 6]
    parts = refs[len(WAYS) + 6 : len(WAYS) + 12]
    keys, vals = refs[len(WAYS) + 12 :]
    rows, cols = q_ref.shape
    keys[:rows] = k_ref[...]
    vals[:rows] = v_ref[...]
    for j in range(len(parts)):
        at = slice(rows + j * BLK, rows + (j + 1) * BLK)
        if j == 5:
            keys[at] = recv[j, 0][0]
            vals[at] = recv[j, 0][1]
            continue

        @pl.when(mine[j] != mine[BIT + j])
        def _(at=at, ref=recv[j, 0]):
            keys[at] = ref[0]
            vals[at] = ref[1]

        @pl.when(mine[j] == mine[BIT + j])
        def _(at=at, ref=recv[j, 1]):
            keys[at] = ref[0]
            vals[at] = ref[1]

    q_rstd = lanes_to_rows(lax.rsqrt(sums_ref[:, :rows] / width + EPS))
    inner = jnp.zeros((rows, HD), jnp.float32)
    for c in range(0, cols, HD):
        at = slice(c, c + HD)
        k = keys[:, at]
        v = vals[:, at]
        q = q_ref[:, at]
        do = do_ref[:, at]
        s = dot(k, q, ((1,), (1,)))
        top = jnp.max(s, axis=0, keepdims=True)
        e = jnp.exp2((s - top) * (SCALE * LOG2E))
        p = e * (1.0 / jnp.sum(e, axis=0, keepdims=True))
        ph = p.astype(jnp.bfloat16)
        attn_t = dot(v.T, ph, ((1,), (0,))).astype(jnp.bfloat16).astype(jnp.float32)
        out_ref[:, at] = attn_t.T.astype(jnp.bfloat16)
        delta = jnp.sum(attn_t * do.astype(jnp.float32).T, axis=0, keepdims=True)
        dp = dot(v, do, ((1,), (1,)))
        ds = (p * (dp - delta)).astype(jnp.bfloat16)
        dq = (dot(k.T, ds, ((1,), (0,))) * SCALE).T
        dq_ref[:, at] = dq
        dk = dot(ds, q, ((1,), (0,))) * SCALE
        dv = dot(ph, do, ((1,), (0,)))
        dk_ref[:, at] = dk[:rows]
        dv_ref[:, at] = dv[:rows]
        dkh = dk[rows:].astype(jnp.bfloat16)
        dvh = dv[rows:].astype(jnp.bfloat16)
        for j, part in enumerate(parts):
            part[0, :, at] = dkh[j * BLK : (j + 1) * BLK]
            part[1, :, at] = dvh[j * BLK : (j + 1) * BLK]
        pull = dq * qpre_ref[:, at].astype(jnp.float32)
        inner += pull * qg_ref[:, at]
        gains_ref[0:1, at] = jnp.sum(pull * q_rstd, axis=0, keepdims=True)
        kf = k.astype(jnp.float32)
        far = jnp.sum(dkh.astype(jnp.float32) * kf[rows:], axis=0, keepdims=True)
        own = jnp.sum(dk[:rows] * kf[:rows], axis=0, keepdims=True)
        gains_ref[1:2, at] = (far + own) / kg_ref[:, at]
    inner_ref[...] = rows_to_lanes(inner)


def collect_kernel(mine, notes, kg_ref, k_ref, *refs):
    count = 2 + len(WAYS)
    fetched = refs[:count]
    dk_out, dv_out, inner_ref, dv_sum, slots, sems = refs[count:]
    into = [dk_out, dv_sum, *(slots.at[i] for i in range(len(WAYS)))]
    copies = [pltpu.make_async_copy(ref, to, sems.at[i]) for i, (ref, to) in enumerate(zip(fetched, into, strict=True))]
    for copy in copies:
        copy.start()
    for copy in copies[:2]:
        copy.wait()
    for i in range(len(WAYS)):
        copies[2 + i].wait()

        @pl.when(is_reader(mine, notes, i))
        def _(i=i):
            at = pl.ds(slot_of(notes[i]), BLK)
            dk_out[at, :] += slots[i, 0].astype(jnp.float32)
            dv_sum[at, :] += slots[i, 1].astype(jnp.float32)

    rows, cols = dk_out.shape
    dv_out[...] = dv_sum[...].astype(jnp.bfloat16)
    inner = jnp.zeros((rows, HD), jnp.float32)
    for c in range(0, cols, HD):
        at = slice(c, c + HD)
        inner += dk_out[:, at] * kg_ref[:, at] * k_ref[:, at].astype(jnp.float32)
    inner_ref[...] = rows_to_lanes(inner)


def back_kernel(width, sums_ref, *refs):
    *refs, dq_out, dk_out = refs
    rows, cols = dq_out.shape
    for i, out in enumerate((dq_out, dk_out)):
        inner_ref, gain_ref, pre_ref, grad_ref = refs[4 * i : 4 * i + 4]
        row_rstd = lax.rsqrt(sums_ref[:, i * rows : (i + 1) * rows] / width + EPS)
        rstd = lanes_to_rows(row_rstd)
        pull = lanes_to_rows(row_rstd * row_rstd * row_rstd * (inner_ref[...] / width))
        for c in range(0, cols, HD):
            at = slice(c, c + HD)
            out[:, at] = (
                rstd * gain_ref[:, at] * grad_ref[:, at] - pre_ref[:, at].astype(jnp.float32) * pull
            ).astype(jnp.bfloat16)


def after(value, *others):
    return lax.optimization_barrier((value, *others))


VMEM = pl.BlockSpec(memory_space=pltpu.VMEM)
SMEM = pl.BlockSpec(memory_space=pltpu.SMEM)
HBM = pl.BlockSpec(memory_space=pltpu.HBM)


def call(kernel, outs, scalars, arrays, name, flops=0, limit=24, scratch=(), far=()):
    size = sum(a.size * a.dtype.itemsize for a in (*arrays, *far)) + sum(o.size * o.dtype.itemsize for o in outs)
    return pl.pallas_call(
        kernel,
        out_shape=outs,
        in_specs=[SMEM] * len(scalars) + [VMEM] * len(arrays) + [HBM] * len(far),
        out_specs=[VMEM] * len(outs),
        scratch_shapes=scratch,
        compiler_params=pltpu.CompilerParams(vmem_limit_bytes=limit * MIB),
        cost_estimate=pl.CostEstimate(flops=flops, bytes_accessed=size, transcendentals=0),
        name=name,
    )(*scalars, *arrays, *far)


def per_device(q_pre, k_pre, values, q_gain, k_gain, grad_out, far_frames, far_blocks):
    rows, cols = q_pre.shape
    width = cols * lax.axis_size("tp")
    bands = far_blocks.shape[1]
    frame = lax.axis_index(CTX)
    rank = lax.axis_index("tp")
    f32, bf16 = jnp.float32, jnp.bfloat16
    struct = jax.ShapeDtypeStruct
    q_gain, k_gain = q_gain[None], k_gain[None]

    *codes, mine = pl.pallas_call(
        notes_kernel,
        out_shape=[struct((1, HD), f32)] * 2 + [struct((16,), jnp.int32)],
        in_specs=[SMEM] * 3,
        out_specs=[VMEM] * 2 + [SMEM],
        name="notes",
    )(jnp.stack([frame, rank]), far_frames, far_blocks)
    lane = jnp.arange(HD)[None]
    notes = jnp.zeros((1, HD), f32)
    for first, code in zip((0, 8), codes):
        pairs = [(a * 8 + t, b * 8 + t) for t, d in enumerate(WAYS[first : first + 8]) for a, b in pairs_of(d)]
        got = lax.ppermute(code, (*CTX, "tp"), pairs)
        notes = notes + jnp.where(lane == first + rank, got, 0.0)
    (squares,) = call(square_kernel, [struct((1, 2 * rows), f32)], [], [q_pre, k_pre], "square")
    squares, notes = lax.psum((squares, notes), "tp")
    notes = notes[0].astype(jnp.int32)
    block = struct((2, BLK, cols), bf16)
    q_normed, k_normed, *sends = call(
        functools.partial(norm_kernel, width),
        [struct((rows, cols), bf16)] * 2 + [block] * len(WAYS),
        [notes],
        [squares, q_gain, k_gain, q_pre, k_pre, values],
        "norm",
    )
    sends = dict(zip(WAYS, sends))
    recvs = {}
    for i, d in enumerate(ORDER):
        if i >= WINDOW:
            early = ORDER[i - WINDOW]
            sends[d], recvs[early] = after(sends[d], recvs[early])
        recvs[d] = move(sends[d], d)
    recvs = [recvs[d] for d in ORDER]
    head = struct((rows, cols), f32)
    far_rows = rows + bands * BLK
    attn, dq, dk, dv, q_inner, gains, *parts = call(
        functools.partial(attention_kernel, width),
        [struct((rows, cols), bf16), head, head, head, struct((1, rows), f32), struct((2, cols), f32)] + [block] * bands,
        [mine],
        [squares, q_gain, k_gain, q_normed, k_normed, values, grad_out, q_pre, *recvs],
        "attention",
        flops=12 * rows * far_rows * cols,
        limit=32,
        scratch=[pltpu.VMEM((far_rows, cols), bf16)] * 2,
    )
    backs = [move(parts[d[0]], d) for d in WAYS]
    gains = lax.psum(lax.psum(gains, "cx"), "cy")
    dk, dv, k_inner = call(
        collect_kernel,
        [head, struct((rows, cols), bf16), struct((1, rows), f32)],
        [mine, notes],
        [k_gain, k_pre],
        "collect",
        limit=60,
        scratch=[
            pltpu.VMEM((rows, cols), f32),
            pltpu.VMEM((len(WAYS), 2, BLK, cols), bf16),
            pltpu.SemaphoreType.DMA((2 + len(WAYS),)),
        ],
        far=[dk, dv, *backs],
    )
    q_inner, k_inner = lax.psum((q_inner, k_inner), "tp")
    dq_pre, dk_pre = call(
        functools.partial(back_kernel, width),
        [struct((rows, cols), bf16)] * 2,
        [],
        [squares, q_inner, q_gain, q_pre, dq, k_inner, k_gain, k_pre, dk],
        "back",
    )
    return (attn, dq_pre, dk_pre, dv, gains[0], gains[1])


def solution(mesh):
    ctx = CTX
    split = Mesh(mesh.devices.reshape(8, 8, 8), (*CTX, "tp"))
    placed = (
        P(ctx, "tp"),
        P(ctx, "tp"),
        P(ctx, "tp"),
        P("tp"),
        P("tp"),
        P(ctx, "tp"),
        P(ctx, None),
        P(ctx, None),
    )
    return jax.shard_map(
        per_device,
        mesh=split,
        in_specs=placed,
        out_specs=(P(ctx, "tp"), P(ctx, "tp"), P(ctx, "tp"), P(ctx, "tp"), P("tp"), P("tp")),
        check_vma=False,
    )
```

```python
import functools

import jax
import jax.numpy as jnp
from jax import lax
from jax.experimental import pallas as pl
from jax.experimental.pallas import tpu as pltpu
from jax.sharding import Mesh
from jax.sharding import PartitionSpec as P

HD = 128
BLK = 128
EPS = 1e-06
SCALE = HD**-0.5
LOG2E = 1.4426950408889634
CTX = ("cy", "cx")
WAYS = tuple((band, other) for band in range(6) for other in range(2 if band < 5 else 1))
MIB = 1 << 20


ORDER = ((4, 0), (4, 1), (5, 0), (2, 0), (2, 1), (3, 0), (3, 1), (1, 0), (1, 1), (0, 0), (0, 1))
WINDOW = 5


def pairs_of(way, count=64):
    band, other = way
    stride = 1 << band
    lower = [f for f in range(count - stride) if (f >> band) & 1 == other]
    return [pair for f in lower for pair in ((f, f + stride), (f + stride, f))]


def move(value, way):
    return lax.ppermute(value, CTX, pairs_of(way))


def dot(a, b, dims):
    return lax.dot_general(a, b, (dims, ((), ())), preferred_element_type=jnp.float32)


def rows_to_lanes(tile):
    return jnp.sum(tile.T, axis=0, keepdims=True)


def lanes_to_rows(row):
    return jnp.broadcast_to(row, (HD, row.shape[1])).T


def square_kernel(q_ref, k_ref, out_ref):
    for i, ref in enumerate((q_ref, k_ref)):
        rows, cols = ref.shape
        total = jnp.zeros((rows, HD), jnp.float32)
        for c in range(0, cols, HD):
            x = ref[:, c : c + HD].astype(jnp.float32)
            total += x * x
        out_ref[:, i * rows : (i + 1) * rows] = rows_to_lanes(total)


def slot_of(note):
    return pl.multiple_of(((note + 1) & 1) * BLK, BLK)


BIT = 8


def is_reader(mine, notes, i):
    band, other = WAYS[i]
    note = notes[i]
    if band == 5:
        return note >= 1
    bit = mine[BIT + band]
    return (note >= 1) & ((note >= 3).astype(jnp.int32) == (1 - bit if other else bit))


def notes_kernel(place, frames, blocks, first_ref, second_ref, mine):
    half = place[1] // 2
    bands = frames.shape[1]
    for ref, band in ((first_ref, half), (second_ref, jnp.minimum(half + 4, bands - 1))):
        code = 1 + blocks[0, band] + 2 * (frames[0, band] > place[0]).astype(jnp.int32)
        ref[...] = jnp.full((1, HD), code, jnp.int32).astype(jnp.float32)
    for j in range(bands):
        mine[j] = (frames[0, j] > place[0]).astype(jnp.int32)
        mine[BIT + j] = (place[0] >> j) & 1


def norm_kernel(width, notes, sums_ref, qg_ref, kg_ref, q_ref, k_ref, v_ref, qn_ref, kn_ref, *sends):
    rows, cols = q_ref.shape
    rstd = lax.rsqrt(sums_ref[...] / width + EPS)
    q_rstd = lanes_to_rows(rstd[:, :rows])
    k_rstd = lanes_to_rows(rstd[:, rows:])
    for c in range(0, cols, HD):
        at = slice(c, c + HD)
        qn_ref[:, at] = (q_ref[:, at].astype(jnp.float32) * q_rstd * qg_ref[:, at]).astype(jnp.bfloat16)
        kn_ref[:, at] = (k_ref[:, at].astype(jnp.float32) * k_rstd * kg_ref[:, at]).astype(jnp.bfloat16)
    for i, send in enumerate(sends):
        start = slot_of(notes[i])
        send[0] = kn_ref[pl.ds(start, BLK), :]
        send[1] = v_ref[pl.ds(start, BLK), :]


def attention_kernel(width, mine, sums_ref, qg_ref, kg_ref, q_ref, k_ref, v_ref, do_ref, qpre_ref, *refs):
    recv = dict(zip(ORDER, refs[: len(WAYS)]))
    out_ref, dq_ref, dk_ref, dv_ref, inner_ref, gains_ref = refs[len(WAYS) : len(WAYS) + 6]
    parts = refs[len(WAYS) + 6 : len(WAYS) + 12]
    keys, vals = refs[len(WAYS) + 12 :]
    rows, cols = q_ref.shape
    keys[:rows] = k_ref[...]
    vals[:rows] = v_ref[...]
    for j in range(len(parts)):
        at = slice(rows + j * BLK, rows + (j + 1) * BLK)
        if j == 5:
            keys[at] = recv[j, 0][0]
            vals[at] = recv[j, 0][1]
            continue

        @pl.when(mine[j] != mine[BIT + j])
        def _(at=at, ref=recv[j, 0]):
            keys[at] = ref[0]
            vals[at] = ref[1]

        @pl.when(mine[j] == mine[BIT + j])
        def _(at=at, ref=recv[j, 1]):
            keys[at] = ref[0]
            vals[at] = ref[1]

    q_rstd = lanes_to_rows(lax.rsqrt(sums_ref[:, :rows] / width + EPS))
    inner = jnp.zeros((rows, HD), jnp.float32)
    for c in range(0, cols, HD):
        at = slice(c, c + HD)
        k = keys[:, at]
        v = vals[:, at]
        q = q_ref[:, at]
        do = do_ref[:, at]
        s = dot(k, q, ((1,), (1,)))
        top = jnp.max(s, axis=0, keepdims=True)
        e = jnp.exp2((s - top) * (SCALE * LOG2E))
        p = e * (1.0 / jnp.sum(e, axis=0, keepdims=True))
        ph = p.astype(jnp.bfloat16)
        attn_t = dot(v, ph, ((0,), (0,))).astype(jnp.bfloat16).astype(jnp.float32)
        out_ref[:, at] = attn_t.T.astype(jnp.bfloat16)
        delta = jnp.sum(attn_t * do.astype(jnp.float32).T, axis=0, keepdims=True)
        dp = dot(v, do, ((1,), (1,)))
        ds = (p * (dp - delta)).astype(jnp.bfloat16)
        dq = (dot(k, ds, ((0,), (0,))) * SCALE).T
        dq_ref[:, at] = dq
        dk = dot(ds, q, ((1,), (0,))) * SCALE
        dv = dot(ph, do, ((1,), (0,)))
        dk_ref[:, at] = dk[:rows]
        dv_ref[:, at] = dv[:rows]
        dkh = dk[rows:].astype(jnp.bfloat16)
        dvh = dv[rows:].astype(jnp.bfloat16)
        for j, part in enumerate(parts):
            part[0, :, at] = dkh[j * BLK : (j + 1) * BLK]
            part[1, :, at] = dvh[j * BLK : (j + 1) * BLK]
        pull = dq * qpre_ref[:, at].astype(jnp.float32)
        inner += pull * qg_ref[:, at]
        gains_ref[0:1, at] = jnp.sum(pull * q_rstd, axis=0, keepdims=True)
        kf = k.astype(jnp.float32)
        far = jnp.sum(dkh.astype(jnp.float32) * kf[rows:], axis=0, keepdims=True)
        own = jnp.sum(dk[:rows] * kf[:rows], axis=0, keepdims=True)
        gains_ref[1:2, at] = (far + own) / kg_ref[:, at]
    inner_ref[...] = rows_to_lanes(inner)


def collect_kernel(mine, notes, kg_ref, k_ref, *refs):
    count = 2 + len(WAYS)
    fetched = refs[:count]
    dk_out, dv_out, inner_ref, dv_sum, slots, sems = refs[count:]
    into = [dk_out, dv_sum, *(slots.at[i] for i in range(len(WAYS)))]
    copies = [pltpu.make_async_copy(ref, to, sems.at[i]) for i, (ref, to) in enumerate(zip(fetched, into, strict=True))]
    for copy in copies:
        copy.start()
    for copy in copies[:2]:
        copy.wait()
    for i in range(len(WAYS)):
        copies[2 + i].wait()

        @pl.when(is_reader(mine, notes, i))
        def _(i=i):
            at = pl.ds(slot_of(notes[i]), BLK)
            dk_out[at, :] += slots[i, 0].astype(jnp.float32)
            dv_sum[at, :] += slots[i, 1].astype(jnp.float32)

    rows, cols = dk_out.shape
    dv_out[...] = dv_sum[...].astype(jnp.bfloat16)
    inner = jnp.zeros((rows, HD), jnp.float32)
    for c in range(0, cols, HD):
        at = slice(c, c + HD)
        inner += dk_out[:, at] * kg_ref[:, at] * k_ref[:, at].astype(jnp.float32)
    inner_ref[...] = rows_to_lanes(inner)


def back_kernel(width, sums_ref, *refs):
    *refs, dq_out, dk_out = refs
    rows, cols = dq_out.shape
    for i, out in enumerate((dq_out, dk_out)):
        inner_ref, gain_ref, pre_ref, grad_ref = refs[4 * i : 4 * i + 4]
        row_rstd = lax.rsqrt(sums_ref[:, i * rows : (i + 1) * rows] / width + EPS)
        rstd = lanes_to_rows(row_rstd)
        pull = lanes_to_rows(row_rstd * row_rstd * row_rstd * (inner_ref[...] / width))
        for c in range(0, cols, HD):
            at = slice(c, c + HD)
            out[:, at] = (
                rstd * gain_ref[:, at] * grad_ref[:, at] - pre_ref[:, at].astype(jnp.float32) * pull
            ).astype(jnp.bfloat16)


def after(value, *others):
    return lax.optimization_barrier((value, *others))


VMEM = pl.BlockSpec(memory_space=pltpu.VMEM)
SMEM = pl.BlockSpec(memory_space=pltpu.SMEM)
HBM = pl.BlockSpec(memory_space=pltpu.HBM)


def call(kernel, outs, scalars, arrays, name, flops=0, limit=24, scratch=(), far=()):
    size = sum(a.size * a.dtype.itemsize for a in (*arrays, *far)) + sum(o.size * o.dtype.itemsize for o in outs)
    return pl.pallas_call(
        kernel,
        out_shape=outs,
        in_specs=[SMEM] * len(scalars) + [VMEM] * len(arrays) + [HBM] * len(far),
        out_specs=[VMEM] * len(outs),
        scratch_shapes=scratch,
        compiler_params=pltpu.CompilerParams(vmem_limit_bytes=limit * MIB),
        cost_estimate=pl.CostEstimate(flops=flops, bytes_accessed=size, transcendentals=0),
        name=name,
    )(*scalars, *arrays, *far)


def per_device(q_pre, k_pre, values, q_gain, k_gain, grad_out, far_frames, far_blocks):
    rows, cols = q_pre.shape
    width = cols * lax.axis_size("tp")
    bands = far_blocks.shape[1]
    frame = lax.axis_index(CTX)
    rank = lax.axis_index("tp")
    f32, bf16 = jnp.float32, jnp.bfloat16
    struct = jax.ShapeDtypeStruct
    q_gain, k_gain = q_gain[None], k_gain[None]

    *codes, mine = pl.pallas_call(
        notes_kernel,
        out_shape=[struct((1, HD), f32)] * 2 + [struct((16,), jnp.int32)],
        in_specs=[SMEM] * 3,
        out_specs=[VMEM] * 2 + [SMEM],
        name="notes",
    )(jnp.stack([frame, rank]), far_frames, far_blocks)
    lane = jnp.arange(HD)[None]
    notes = jnp.zeros((1, HD), f32)
    for first, code in zip((0, 8), codes):
        pairs = [(a * 8 + t, b * 8 + t) for t, d in enumerate(WAYS[first : first + 8]) for a, b in pairs_of(d)]
        got = lax.ppermute(code, (*CTX, "tp"), pairs)
        notes = notes + jnp.where(lane == first + rank, got, 0.0)
    (squares,) = call(square_kernel, [struct((1, 2 * rows), f32)], [], [q_pre, k_pre], "square")
    squares, notes = lax.psum((squares, notes), "tp")
    notes = notes[0].astype(jnp.int32)
    block = struct((2, BLK, cols), bf16)
    q_normed, k_normed, *sends = call(
        functools.partial(norm_kernel, width),
        [struct((rows, cols), bf16)] * 2 + [block] * len(WAYS),
        [notes],
        [squares, q_gain, k_gain, q_pre, k_pre, values],
        "norm",
    )
    sends = dict(zip(WAYS, sends))
    recvs = {}
    for i, d in enumerate(ORDER):
        if i >= WINDOW:
            early = ORDER[i - WINDOW]
            sends[d], recvs[early] = after(sends[d], recvs[early])
        recvs[d] = move(sends[d], d)
    recvs = [recvs[d] for d in ORDER]
    head = struct((rows, cols), f32)
    far_rows = rows + bands * BLK
    attn, dq, dk, dv, q_inner, gains, *parts = call(
        functools.partial(attention_kernel, width),
        [struct((rows, cols), bf16), head, head, head, struct((1, rows), f32), struct((2, cols), f32)] + [block] * bands,
        [mine],
        [squares, q_gain, k_gain, q_normed, k_normed, values, grad_out, q_pre, *recvs],
        "attention",
        flops=12 * rows * far_rows * cols,
        limit=46,
        scratch=[pltpu.VMEM((far_rows, cols), bf16)] * 2,
    )
    backs = [move(parts[d[0]], d) for d in WAYS]
    gains = lax.psum(lax.psum(gains, "cx"), "cy")
    dk, dv, k_inner = call(
        collect_kernel,
        [head, struct((rows, cols), bf16), struct((1, rows), f32)],
        [mine, notes],
        [k_gain, k_pre],
        "collect",
        limit=60,
        scratch=[
            pltpu.VMEM((rows, cols), f32),
            pltpu.VMEM((len(WAYS), 2, BLK, cols), bf16),
            pltpu.SemaphoreType.DMA((2 + len(WAYS),)),
        ],
        far=[dk, dv, *backs],
    )
    q_inner, k_inner = lax.psum((q_inner, k_inner), "tp")
    dq_pre, dk_pre = call(
        functools.partial(back_kernel, width),
        [struct((rows, cols), bf16)] * 2,
        [],
        [squares, q_inner, q_gain, q_pre, dq, k_inner, k_gain, k_pre, dk],
        "back",
    )
    return (attn, dq_pre, dk_pre, dv, gains[0], gains[1])


def solution(mesh):
    ctx = CTX
    split = Mesh(mesh.devices.reshape(8, 8, 8), (*CTX, "tp"))
    placed = (
        P(ctx, "tp"),
        P(ctx, "tp"),
        P(ctx, "tp"),
        P("tp"),
        P("tp"),
        P(ctx, "tp"),
        P(ctx, None),
        P(ctx, None),
    )
    return jax.shard_map(
        per_device,
        mesh=split,
        in_specs=placed,
        out_specs=(P(ctx, "tp"), P(ctx, "tp"), P(ctx, "tp"), P(ctx, "tp"), P("tp"), P("tp")),
        check_vma=False,
    )
```

```python
import functools

import jax
import jax.numpy as jnp
from jax import lax
from jax.experimental import pallas as pl
from jax.experimental.pallas import tpu as pltpu
from jax.sharding import Mesh
from jax.sharding import PartitionSpec as P

HD = 128
BLK = 128
EPS = 1e-06
SCALE = HD**-0.5
LOG2E = 1.4426950408889634
CTX = ("cy", "cx")
WAYS = tuple((band, other) for band in range(6) for other in range(2 if band < 5 else 1))
MIB = 1 << 20


ORDER = ((4, 0), (4, 1), (5, 0), (2, 0), (2, 1), (3, 0), (3, 1), (1, 0), (1, 1), (0, 0), (0, 1))
WINDOW = 6


def pairs_of(way, count=64):
    band, other = way
    stride = 1 << band
    lower = [f for f in range(count - stride) if (f >> band) & 1 == other]
    return [pair for f in lower for pair in ((f, f + stride), (f + stride, f))]


def move(value, way):
    return lax.ppermute(value, CTX, pairs_of(way))


def dot(a, b, dims):
    return lax.dot_general(a, b, (dims, ((), ())), preferred_element_type=jnp.float32)


def rows_to_lanes(tile):
    return jnp.sum(tile.T, axis=0, keepdims=True)


def lanes_to_rows(row):
    return jnp.broadcast_to(row, (HD, row.shape[1])).T


def square_kernel(q_ref, k_ref, out_ref):
    for i, ref in enumerate((q_ref, k_ref)):
        rows, cols = ref.shape
        total = jnp.zeros((rows, HD), jnp.float32)
        for c in range(0, cols, HD):
            x = ref[:, c : c + HD].astype(jnp.float32)
            total += x * x
        out_ref[:, i * rows : (i + 1) * rows] = rows_to_lanes(total)


def slot_of(note):
    return pl.multiple_of(((note + 1) & 1) * BLK, BLK)


BIT = 8


def is_reader(mine, notes, i):
    band, other = WAYS[i]
    note = notes[i]
    if band == 5:
        return note >= 1
    bit = mine[BIT + band]
    return (note >= 1) & ((note >= 3).astype(jnp.int32) == (1 - bit if other else bit))


def notes_kernel(place, frames, blocks, first_ref, second_ref, mine):
    half = place[1] // 2
    bands = frames.shape[1]
    for ref, band in ((first_ref, half), (second_ref, jnp.minimum(half + 4, bands - 1))):
        code = 1 + blocks[0, band] + 2 * (frames[0, band] > place[0]).astype(jnp.int32)
        ref[...] = jnp.full((1, HD), code, jnp.int32).astype(jnp.float32)
    for j in range(bands):
        mine[j] = (frames[0, j] > place[0]).astype(jnp.int32)
        mine[BIT + j] = (place[0] >> j) & 1


def norm_kernel(width, notes, sums_ref, qg_ref, kg_ref, q_ref, k_ref, v_ref, qn_ref, kn_ref, *sends):
    rows, cols = q_ref.shape
    rstd = lax.rsqrt(sums_ref[...] / width + EPS)
    q_rstd = lanes_to_rows(rstd[:, :rows])
    k_rstd = lanes_to_rows(rstd[:, rows:])
    for c in range(0, cols, HD):
        at = slice(c, c + HD)
        qn_ref[:, at] = (q_ref[:, at].astype(jnp.float32) * q_rstd * qg_ref[:, at]).astype(jnp.bfloat16)
        kn_ref[:, at] = (k_ref[:, at].astype(jnp.float32) * k_rstd * kg_ref[:, at]).astype(jnp.bfloat16)
    for i, send in enumerate(sends):
        start = slot_of(notes[i])
        send[0] = kn_ref[pl.ds(start, BLK), :]
        send[1] = v_ref[pl.ds(start, BLK), :]


def attention_kernel(width, mine, sums_ref, qg_ref, kg_ref, q_ref, k_ref, v_ref, do_ref, qpre_ref, *refs):
    recv = dict(zip(ORDER, refs[: len(WAYS)]))
    out_ref, dq_ref, dk_ref, dv_ref, inner_ref, gains_ref = refs[len(WAYS) : len(WAYS) + 6]
    parts = refs[len(WAYS) + 6 : len(WAYS) + 12]
    keys, vals = refs[len(WAYS) + 12 :]
    rows, cols = q_ref.shape
    keys[:rows] = k_ref[...]
    vals[:rows] = v_ref[...]
    for j in range(len(parts)):
        at = slice(rows + j * BLK, rows + (j + 1) * BLK)
        if j == 5:
            keys[at] = recv[j, 0][0]
            vals[at] = recv[j, 0][1]
            continue

        @pl.when(mine[j] != mine[BIT + j])
        def _(at=at, ref=recv[j, 0]):
            keys[at] = ref[0]
            vals[at] = ref[1]

        @pl.when(mine[j] == mine[BIT + j])
        def _(at=at, ref=recv[j, 1]):
            keys[at] = ref[0]
            vals[at] = ref[1]

    q_rstd = lanes_to_rows(lax.rsqrt(sums_ref[:, :rows] / width + EPS))
    inner = jnp.zeros((rows, HD), jnp.float32)
    for c in range(0, cols, HD):
        at = slice(c, c + HD)
        k = keys[:, at]
        v = vals[:, at]
        q = q_ref[:, at]
        do = do_ref[:, at]
        s = dot(k, q, ((1,), (1,)))
        top = jnp.max(s, axis=0, keepdims=True)
        e = jnp.exp2((s - top) * (SCALE * LOG2E))
        p = e * (1.0 / jnp.sum(e, axis=0, keepdims=True))
        ph = p.astype(jnp.bfloat16)
        attn_t = dot(v, ph, ((0,), (0,))).astype(jnp.bfloat16).astype(jnp.float32)
        out_ref[:, at] = attn_t.T.astype(jnp.bfloat16)
        delta = jnp.sum(attn_t * do.astype(jnp.float32).T, axis=0, keepdims=True)
        dp = dot(v, do, ((1,), (1,)))
        ds = (p * (dp - delta)).astype(jnp.bfloat16)
        dq = (dot(k, ds, ((0,), (0,))) * SCALE).T
        dq_ref[:, at] = dq
        dk = dot(ds, q, ((1,), (0,))) * SCALE
        dv = dot(ph, do, ((1,), (0,)))
        dk_ref[:, at] = dk[:rows]
        dv_ref[:, at] = dv[:rows]
        dkh = dk[rows:].astype(jnp.bfloat16)
        dvh = dv[rows:].astype(jnp.bfloat16)
        for j, part in enumerate(parts):
            part[0, :, at] = dkh[j * BLK : (j + 1) * BLK]
            part[1, :, at] = dvh[j * BLK : (j + 1) * BLK]
        pull = dq * qpre_ref[:, at].astype(jnp.float32)
        inner += pull * qg_ref[:, at]
        gains_ref[0:1, at] = jnp.sum(pull * q_rstd, axis=0, keepdims=True)
        kf = k.astype(jnp.float32)
        far = jnp.sum(dkh.astype(jnp.float32) * kf[rows:], axis=0, keepdims=True)
        own = jnp.sum(dk[:rows] * kf[:rows], axis=0, keepdims=True)
        gains_ref[1:2, at] = (far + own) / kg_ref[:, at]
    inner_ref[...] = rows_to_lanes(inner)


def collect_kernel(mine, notes, kg_ref, k_ref, *refs):
    count = 2 + len(WAYS)
    fetched = refs[:count]
    dk_out, dv_out, inner_ref, dv_sum, slots, sems = refs[count:]
    into = [dk_out, dv_sum, *(slots.at[i] for i in range(len(WAYS)))]
    copies = [pltpu.make_async_copy(ref, to, sems.at[i]) for i, (ref, to) in enumerate(zip(fetched, into, strict=True))]
    for copy in copies:
        copy.start()
    for copy in copies[:2]:
        copy.wait()
    for i in range(len(WAYS)):
        copies[2 + i].wait()

        @pl.when(is_reader(mine, notes, i))
        def _(i=i):
            at = pl.ds(slot_of(notes[i]), BLK)
            dk_out[at, :] += slots[i, 0].astype(jnp.float32)
            dv_sum[at, :] += slots[i, 1].astype(jnp.float32)

    rows, cols = dk_out.shape
    dv_out[...] = dv_sum[...].astype(jnp.bfloat16)
    inner = jnp.zeros((rows, HD), jnp.float32)
    for c in range(0, cols, HD):
        at = slice(c, c + HD)
        inner += dk_out[:, at] * kg_ref[:, at] * k_ref[:, at].astype(jnp.float32)
    inner_ref[...] = rows_to_lanes(inner)


def back_kernel(width, sums_ref, *refs):
    *refs, dq_out, dk_out = refs
    rows, cols = dq_out.shape
    for i, out in enumerate((dq_out, dk_out)):
        inner_ref, gain_ref, pre_ref, grad_ref = refs[4 * i : 4 * i + 4]
        row_rstd = lax.rsqrt(sums_ref[:, i * rows : (i + 1) * rows] / width + EPS)
        rstd = lanes_to_rows(row_rstd)
        pull = lanes_to_rows(row_rstd * row_rstd * row_rstd * (inner_ref[...] / width))
        for c in range(0, cols, HD):
            at = slice(c, c + HD)
            out[:, at] = (
                rstd * gain_ref[:, at] * grad_ref[:, at] - pre_ref[:, at].astype(jnp.float32) * pull
            ).astype(jnp.bfloat16)


def after(value, *others):
    return lax.optimization_barrier((value, *others))


VMEM = pl.BlockSpec(memory_space=pltpu.VMEM)
SMEM = pl.BlockSpec(memory_space=pltpu.SMEM)
HBM = pl.BlockSpec(memory_space=pltpu.HBM)


def call(kernel, outs, scalars, arrays, name, flops=0, limit=24, scratch=(), far=()):
    size = sum(a.size * a.dtype.itemsize for a in (*arrays, *far)) + sum(o.size * o.dtype.itemsize for o in outs)
    return pl.pallas_call(
        kernel,
        out_shape=outs,
        in_specs=[SMEM] * len(scalars) + [VMEM] * len(arrays) + [HBM] * len(far),
        out_specs=[VMEM] * len(outs),
        scratch_shapes=scratch,
        compiler_params=pltpu.CompilerParams(vmem_limit_bytes=limit * MIB),
        cost_estimate=pl.CostEstimate(flops=flops, bytes_accessed=size, transcendentals=0),
        name=name,
    )(*scalars, *arrays, *far)


def per_device(q_pre, k_pre, values, q_gain, k_gain, grad_out, far_frames, far_blocks):
    rows, cols = q_pre.shape
    width = cols * lax.axis_size("tp")
    bands = far_blocks.shape[1]
    frame = lax.axis_index(CTX)
    rank = lax.axis_index("tp")
    f32, bf16 = jnp.float32, jnp.bfloat16
    struct = jax.ShapeDtypeStruct
    q_gain, k_gain = q_gain[None], k_gain[None]

    *codes, mine = pl.pallas_call(
        notes_kernel,
        out_shape=[struct((1, HD), f32)] * 2 + [struct((16,), jnp.int32)],
        in_specs=[SMEM] * 3,
        out_specs=[VMEM] * 2 + [SMEM],
        name="notes",
    )(jnp.stack([frame, rank]), far_frames, far_blocks)
    lane = jnp.arange(HD)[None]
    notes = jnp.zeros((1, HD), f32)
    for first, code in zip((0, 8), codes):
        pairs = [(a * 8 + t, b * 8 + t) for t, d in enumerate(WAYS[first : first + 8]) for a, b in pairs_of(d)]
        got = lax.ppermute(code, (*CTX, "tp"), pairs)
        notes = notes + jnp.where(lane == first + rank, got, 0.0)
    (squares,) = call(square_kernel, [struct((1, 2 * rows), f32)], [], [q_pre, k_pre], "square")
    squares, notes = lax.psum((squares, notes), "tp")
    notes = notes[0].astype(jnp.int32)
    block = struct((2, BLK, cols), bf16)
    q_normed, k_normed, *sends = call(
        functools.partial(norm_kernel, width),
        [struct((rows, cols), bf16)] * 2 + [block] * len(WAYS),
        [notes],
        [squares, q_gain, k_gain, q_pre, k_pre, values],
        "norm",
    )
    sends = dict(zip(WAYS, sends))
    recvs = {}
    for i, d in enumerate(ORDER):
        if i >= WINDOW:
            early = ORDER[i - WINDOW]
            sends[d], recvs[early] = after(sends[d], recvs[early])
        recvs[d] = move(sends[d], d)
    recvs = [recvs[d] for d in ORDER]
    head = struct((rows, cols), f32)
    far_rows = rows + bands * BLK
    attn, dq, dk, dv, q_inner, gains, *parts = call(
        functools.partial(attention_kernel, width),
        [struct((rows, cols), bf16), head, head, head, struct((1, rows), f32), struct((2, cols), f32)] + [block] * bands,
        [mine],
        [squares, q_gain, k_gain, q_normed, k_normed, values, grad_out, q_pre, *recvs],
        "attention",
        flops=12 * rows * far_rows * cols,
        limit=46,
        scratch=[pltpu.VMEM((far_rows, cols), bf16)] * 2,
    )
    backs = [move(parts[d[0]], d) for d in WAYS]
    gains = lax.psum(lax.psum(gains, "cx"), "cy")
    dk, dv, k_inner = call(
        collect_kernel,
        [head, struct((rows, cols), bf16), struct((1, rows), f32)],
        [mine, notes],
        [k_gain, k_pre],
        "collect",
        limit=60,
        scratch=[
            pltpu.VMEM((rows, cols), f32),
            pltpu.VMEM((len(WAYS), 2, BLK, cols), bf16),
            pltpu.SemaphoreType.DMA((2 + len(WAYS),)),
        ],
        far=[dk, dv, *backs],
    )
    q_inner, k_inner = lax.psum((q_inner, k_inner), "tp")
    gains, k_inner = after(gains, k_inner)
    dq_pre, dk_pre = call(
        functools.partial(back_kernel, width),
        [struct((rows, cols), bf16)] * 2,
        [],
        [squares, q_inner, q_gain, q_pre, dq, k_inner, k_gain, k_pre, dk],
        "back",
    )
    return (attn, dq_pre, dk_pre, dv, gains[0], gains[1])


def solution(mesh):
    ctx = CTX
    split = Mesh(mesh.devices.reshape(8, 8, 8), (*CTX, "tp"))
    placed = (
        P(ctx, "tp"),
        P(ctx, "tp"),
        P(ctx, "tp"),
        P("tp"),
        P("tp"),
        P(ctx, "tp"),
        P(ctx, None),
        P(ctx, None),
    )
    return jax.shard_map(
        per_device,
        mesh=split,
        in_specs=placed,
        out_specs=(P(ctx, "tp"), P(ctx, "tp"), P(ctx, "tp"), P(ctx, "tp"), P("tp"), P("tp")),
        check_vma=False,
    )
```
